512 devices in a mesh: head: 32 (over z, core), req: 16 (over y, x).
Axes of the slice: x: 4, y: 4, z: 16, core: 2. Of those that a mesh axis runs over, the one named last changes fastest.
Arguments:
- queries: bfloat16 [65536, 4096], P(('req', 'head')), parts along dimension 0, may hold values from -120 to 120
- keys_new: bfloat16 [65536, 1024], P(('req', 'head')), parts along dimension 0, may hold values from -6 to 6
- values_new: bfloat16 [65536, 1024], P(('req', 'head')), parts along dimension 0, may hold values from -18 to 18
- prefix_keys: bfloat16 [262144, 1024], P(('req', 'head')), parts along dimension 0, may hold values from -6 to 6
- prefix_values: bfloat16 [262144, 1024], P(('req', 'head')), parts along dimension 0, may hold values from -18 to 18
- vertical_blocks: int32 [512, 32], P('req'), parts along dimension 0, may hold values from 0 to 255, as said below
- vertical_counts: int32 [512], P('req'), parts along dimension 0, may hold values from 4 to 32, as said below
- slash_offsets: int32 [512, 8], P('req'), parts along dimension 0, may hold values from 0 to 63, as said below
- slash_counts: int32 [512], P('req'), parts along dimension 0, may hold values from 1 to 8
Outputs:
- attended: bfloat16 [65536, 4096], P(('req', 'head')), parts along dimension 0
The draws below stay inside these ranges and needn't reach their ends.
There are 16 independent parts, one for each index of `req`. The reference program is written for one: setup_inputs(seed, part) draws one part's arguments, and reference() takes and returns one part's arrays. A program takes and returns all parts, laid end to end along the dimension named above; each array names one. Nothing has to cross between parts.
Inputs may be any that keep to these rules, and one draw needn't show every extreme that they name: `vertical_blocks`: the 32 entries of one head's list lie in distinct ranges of 8 blocks (range r holds blocks r * 8 to (r + 1) * 8 - 1), so each range holds at most one; unused entries are valid blocks too; some head lists a block in every range. `vertical_counts`: one head uses all 32 entries. `slash_offsets`: each head's first offset is 0 and its offsets are distinct.
All inputs are finite; a program needn't handle non-finite values.
Results may differ from the reference program's by a relative error of at most 0.0039.
Values may be sent and summed in bfloat16 or wider, within the bound.
A program may use at most 64 MiB of HBM per device.

```python
import math
import jax
import jax.numpy as jnp
from jax import lax

H = 32
KVH = 8
HD = 128
BLK = 64
SMAX = 8
SPAN = 4096
QBLOCKS = 64
PREFIX = 16384
PBLOCKS = 256
OWN_BLOCKS = 8
SLOTS = 32


def chosen_heads(key):
    shuffled = jax.random.permutation(jax.random.fold_in(key, 77), H)
    return (shuffled[0], shuffled[1])


def strong_rows(key):
    base_keys = jnp.clip(jax.random.normal(jax.random.fold_in(key, 92), (SPAN, KVH * HD), jnp.float32), -6.0, 6.0)
    return base_keys


def draw_queries(key, part):
    key = jax.random.fold_in(key, 31)
    drawn = jnp.clip(jax.random.normal(key, (SPAN, H * HD), jnp.float32), -6.0, 6.0) * 1.5
    return drawn.astype(jnp.bfloat16)


def draw_keys_new(key, part):
    base_keys = strong_rows(key)
    return base_keys.astype(jnp.bfloat16)


def draw_vertical_blocks(key, part):
    busiest, lightest = chosen_heads(key)
    key = jax.random.fold_in(key, 11)
    head_keys = jax.random.split(key, H)
    owners = jax.vmap(lambda subkey: jax.random.permutation(subkey, SLOTS))(head_keys)
    offsets = jax.random.randint(jax.random.fold_in(key, 5), (H, SLOTS), 0, OWN_BLOCKS)
    by_entry = jnp.take_along_axis(offsets, owners, 1)
    head_ids = jnp.arange(H)[:, None]
    lowest = (head_ids == busiest) & (owners == 0)
    highest = (head_ids == busiest) & (owners == SLOTS - 1)
    by_entry = jnp.where(lowest, 0, jnp.where(highest, OWN_BLOCKS - 1, by_entry))
    return (owners * OWN_BLOCKS + by_entry).astype(jnp.int32)


def draw_vertical_counts(key, part):
    busiest, lightest = chosen_heads(key)
    key = jax.random.fold_in(key, 12)
    halvings = jax.random.randint(key, (H,), 0, 4)
    head_ids = jnp.arange(H)
    halvings = jnp.where(head_ids == busiest, 0, jnp.where(head_ids == lightest, 3, halvings))
    return jnp.maximum(1, SLOTS // 2 ** halvings).astype(jnp.int32)


def draw_slash_offsets(key, part):
    busiest, lightest = chosen_heads(key)
    key = jax.random.fold_in(key, 13)
    head_keys = jax.random.split(key, H)
    remaining = jax.vmap(lambda subkey: jax.random.permutation(subkey, QBLOCKS - 1))(head_keys)[:, :SMAX - 1]
    first_entry = remaining[:, :1]
    shifted = (remaining - first_entry + QBLOCKS - 2) % (QBLOCKS - 1)
    remaining = jnp.where(jnp.arange(H)[:, None] == busiest, shifted, remaining)
    return jnp.concatenate([jnp.zeros((H, 1), jnp.int32), (remaining + 1).astype(jnp.int32)], 1)


def draw_slash_counts(key, part):
    busiest, lightest = chosen_heads(key)
    key = jax.random.fold_in(key, 14)
    drawn = jax.random.randint(key, (H,), 1, SMAX + 1)
    head_ids = jnp.arange(H)
    return jnp.where(head_ids == busiest, SMAX, jnp.where(head_ids == lightest, 1, drawn)).astype(jnp.int32)


def shard_levels(rng, extent, pieces, low, top_value):
    def one(axis_at, shards_of):
        heights = jax.random.uniform(jax.random.fold_in(jax.random.fold_in(rng, 6), axis_at), (shards_of,), jnp.float32, low / len(pieces), top_value / len(pieces))
        return jnp.repeat(jnp.exp(heights), extent[axis_at] // shards_of).reshape((-1,) + (1,) * (len(extent) - axis_at - 1))

    level = one(*pieces[0])
    for cut in pieces[1:]:
        level = level * one(*cut)
    return level


def scatter_about(stream_key, extent, width, bound, cuts=(), kind=jnp.bfloat16):
    values = width * jax.random.normal(stream_key, extent, jnp.float32)
    if cuts:
        values = values * shard_levels(stream_key, extent, cuts, -0.22, 0.18)
    return jnp.clip(values, -bound, bound).astype(kind)


def setup_inputs(seed: int = 0, part: int = 0) -> dict:
    keys = jax.random.split(jax.random.key(seed), 10)
    own_keys = jax.random.split(jax.random.fold_in(keys[9], part), 10)
    queries = draw_queries(jax.random.fold_in(jax.random.fold_in(keys[9], part), 71), part)
    keys_new = draw_keys_new(jax.random.fold_in(jax.random.fold_in(keys[9], part), 71), part)
    values_new = scatter_about(own_keys[2], (SPAN, KVH * HD), 3.0, 18.0, ((0, 32),))
    prefix_keys = scatter_about(own_keys[3], (PREFIX, KVH * HD), 1.0, 6.0, ((0, 32),))
    prefix_values = scatter_about(own_keys[4], (PREFIX, KVH * HD), 3.0, 18.0, ((0, 32),))
    vertical_blocks = draw_vertical_blocks(jax.random.fold_in(jax.random.fold_in(keys[9], part), 71), part)
    vertical_counts = draw_vertical_counts(jax.random.fold_in(jax.random.fold_in(keys[9], part), 71), part)
    slash_offsets = draw_slash_offsets(jax.random.fold_in(jax.random.fold_in(keys[9], part), 71), part)
    slash_counts = draw_slash_counts(jax.random.fold_in(jax.random.fold_in(keys[9], part), 71), part)
    return {"queries": queries, "keys_new": keys_new, "values_new": values_new, "prefix_keys": prefix_keys, "prefix_values": prefix_values, "vertical_blocks": vertical_blocks, "vertical_counts": vertical_counts, "slash_offsets": slash_offsets, "slash_counts": slash_counts}


def attend_head(head_index, queries, keys_new, values_new, prefix_keys, prefix_values, vertical_blocks, vertical_counts, slash_offsets, slash_counts):
    group_size = H // KVH
    kv_head = head_index // group_size
    score_scale = 1.0 / math.sqrt(HD)
    q_head = lax.dynamic_slice_in_dim(queries, head_index * HD, HD, 1)
    k_head = lax.dynamic_slice_in_dim(keys_new, kv_head * HD, HD, 1)
    v_head = lax.dynamic_slice_in_dim(values_new, kv_head * HD, HD, 1)
    prefix_k = lax.dynamic_slice_in_dim(prefix_keys, kv_head * HD, HD, 1)
    prefix_v = lax.dynamic_slice_in_dim(prefix_values, kv_head * HD, HD, 1)
    listed = vertical_blocks[head_index]
    far_keys = prefix_k.reshape(PBLOCKS, BLK, HD)[listed].reshape(SLOTS * BLK, HD)
    far_values = prefix_v.reshape(PBLOCKS, BLK, HD)[listed].reshape(SLOTS * BLK, HD)
    far_live = jnp.repeat(jnp.arange(SLOTS, dtype=jnp.int32) < vertical_counts[head_index], BLK)
    offsets = slash_offsets[head_index]
    target = jnp.arange(QBLOCKS, dtype=jnp.int32)[:, None] - offsets[None, :]
    usable = (target >= 0) & (jnp.arange(SMAX, dtype=jnp.int32)[None, :] < slash_counts[head_index])
    picked = jnp.maximum(target, 0)
    near_keys = k_head.reshape(QBLOCKS, BLK, HD)[picked].reshape(QBLOCKS, SMAX * BLK, HD)
    near_values = v_head.reshape(QBLOCKS, BLK, HD)[picked].reshape(QBLOCKS, SMAX * BLK, HD)
    within = jnp.arange(BLK)[None, :] <= jnp.arange(BLK)[:, None]
    allowed = usable[:, None, :, None] & (within[None, :, None, :] | (offsets != 0)[None, None, :, None])
    allowed = allowed.reshape(QBLOCKS, BLK, SMAX * BLK)
    far_scores = jnp.dot(q_head, far_keys.T, preferred_element_type=jnp.float32) * score_scale
    far_scores = jnp.where(far_live[None, :], far_scores, -jnp.inf).reshape(QBLOCKS, BLK, SLOTS * BLK)
    near_scores = jnp.einsum('qrd,qkd->qrk', q_head.reshape(QBLOCKS, BLK, HD).astype(jnp.float32), near_keys.astype(jnp.float32)) * score_scale
    near_scores = jnp.where(allowed, near_scores, -jnp.inf)
    row_top = jnp.maximum(lax.optimization_barrier(jnp.max(far_scores, 2)), lax.optimization_barrier(jnp.max(near_scores, 2)))
    far_weights = jnp.exp(far_scores - row_top[..., None])
    near_weights = jnp.exp(near_scores - row_top[..., None])
    row_total = lax.optimization_barrier(jnp.sum(far_weights, 2)) + lax.optimization_barrier(jnp.sum(near_weights, 2))
    far_rounded = lax.optimization_barrier(far_weights.astype(jnp.bfloat16))
    near_rounded = lax.optimization_barrier(near_weights.astype(jnp.bfloat16))
    mixed_rows = jnp.dot(far_rounded.reshape(SPAN, SLOTS * BLK), far_values, preferred_element_type=jnp.float32).reshape(QBLOCKS, BLK, HD)
    mixed_rows = mixed_rows + jnp.einsum('qrk,qkd->qrd', near_rounded.astype(jnp.float32), near_values.astype(jnp.float32))
    return (mixed_rows / row_total[..., None]).reshape(SPAN, HD).astype(jnp.bfloat16)

def reference(queries, keys_new, values_new, prefix_keys, prefix_values, vertical_blocks, vertical_counts, slash_offsets, slash_counts):

    def one_head(head_index):
        return attend_head(head_index, queries, keys_new, values_new, prefix_keys, prefix_values, vertical_blocks, vertical_counts, slash_offsets, slash_counts)
    per_head = lax.map(one_head, jnp.arange(H, dtype=jnp.int32))
    return jnp.transpose(per_head, (1, 0, 2)).reshape(SPAN, H * HD)
```

```python
import math

import jax
import jax.numpy as jnp
from jax import lax
from jax.experimental import pallas as pl
from jax.experimental.pallas import tpu as pltpu
from jax.sharding import PartitionSpec as P

H = 32
KVH = 8
HD = 128
BLK = 64
SMAX = 8
DEV = 32
CHIPS = 16
OWN = 8
TOK = 128
FAR = DEV * BLK
NEAR = SMAX * BLK
MESH = pl.DeviceIdType.MESH
SCALE = math.log2(math.e) / math.sqrt(HD)
NEG = -math.inf


def kernel(
    q,
    k,
    v,
    pk,
    pv,
    vb,
    vc,
    so,
    sc,
    out,
    kv,
    far,
    far_send,
    pkb,
    pvb,
    qb,
    ob,
    far_bias,
    tri,
    load_sem,
    near_sem,
    near_send_sem,
    far_sem,
    far_send_sem,
    q_sem,
    q_send_sem,
    out_sem,
    out_send_sem,
):
    me = lax.axis_index("head")
    z, c = lax.div(me, 2), lax.rem(me, 2)
    g, odd = lax.div(z, 2), lax.rem(z, 2)
    sibling = 2 * z + 1 - c
    across = 2 * (2 * g + 1 - odd) + c

    def columns(index):
        return pl.ds(pl.multiple_of(index * HD, HD), HD)

    def remote(src, dst, send_sem, recv_sem, device):
        return pltpu.make_async_remote_copy(
            src_ref=src,
            dst_ref=dst,
            send_sem=send_sem,
            recv_sem=recv_sem,
            device_id={"head": device},
            device_id_type=MESH,
        )

    def wait_bytes(ref, sem):
        pltpu.make_async_copy(ref, ref, sem).wait()

    barrier = pltpu.get_barrier_semaphore()

    def greet(j, carry):
        pl.semaphore_signal(
            barrier, inc=1, device_id={"head": lax.rem(me + j, DEV)}, device_id_type=MESH
        )
        return carry

    lax.fori_loop(1, DEV, greet, 0)
    load_k = pltpu.make_async_copy(pk, pkb, load_sem.at[0])
    load_v = pltpu.make_async_copy(pv, pvb, load_sem.at[1])
    load_k.start()
    load_v.start()

    spot = 15 * (1 - odd)
    own_k = pltpu.make_async_copy(k.at[:, :, columns(g)], kv.at[c, spot, 0], load_sem.at[2])
    own_v = pltpu.make_async_copy(v.at[:, :, columns(g)], kv.at[c, spot, 1], load_sem.at[3])
    own_k.start()
    own_v.start()
    pltpu.make_async_copy(q.at[:, columns(me)], qb.at[me], q_sem.at[z]).start()

    pl.semaphore_wait(barrier, DEV - 1)

    def near_out(j, carry):
        group = lax.rem(g + j, KVH)
        chip = 2 * group + lax.div(lax.rem(2 * group - z + CHIPS, CHIPS), CHIPS // 2)
        place = lax.rem(z - 2 * group - 1 + 2 * CHIPS, CHIPS)
        for part, source in enumerate((k, v)):
            remote(
                source.at[:, :, columns(group)],
                kv.at[c, place, part],
                near_send_sem.at[0],
                near_sem.at[0],
                2 * chip + c,
            ).start()
        return carry

    lax.fori_loop(1, KVH, near_out, 0)

    load_k.wait()
    load_v.wait()

    def picked(head):
        block = jnp.int32(0)
        count = vc[head]
        for t in range(DEV):
            entry = vb[head, t]
            mine = (lax.shift_right_logical(entry, 3) == me) & (t < count)
            block = block + jnp.where(mine, entry - OWN * me, 0)
        return block

    def pick(head, buffer, slot):
        block = picked(head)
        cols = columns(lax.div(head, H // KVH))
        buffer[slot, 0] = pkb[block, :, cols]
        buffer[slot, 1] = pvb[block, :, cols]

    def far_out(j, carry):
        head = lax.rem(me + j, DEV)
        pick(head, far_send, head)
        remote(far_send.at[head], far.at[me], far_send_sem, far_sem, head).start()
        return carry

    lax.fori_loop(1, DEV, far_out, 0)
    pick(me, far, me)

    own_k.wait()
    own_v.wait()
    first = OWN * (1 - odd)
    other = OWN * odd
    mine = kv.at[c, pl.ds(first, OWN)]
    wait_bytes(kv.at[c, pl.ds(first, OWN - 1)], near_sem.at[0])
    remote(mine, mine, near_send_sem.at[1], near_sem.at[1], sibling).start()
    remote(mine, mine, near_send_sem.at[2], near_sem.at[2], across).start()

    def q_out(j, carry):
        head = lax.rem(me - j + DEV, DEV)
        remote(q.at[:, columns(head)], qb.at[me], q_send_sem, q_sem.at[z], head).start()
        return carry

    lax.fori_loop(1, DEV, q_out, 0)

    count = vc[me]
    lane = lax.broadcasted_iota(jnp.int32, (1, FAR), 1)
    slot = lax.shift_right_logical(lane, 6)
    live = jnp.zeros((1, FAR), jnp.int32)
    for t in range(DEV):
        owner = jnp.where(t < count, lax.shift_right_logical(vb[me, t], 3), -1)
        live = jnp.where(slot == owner, 1, live)
    far_bias[...] = jnp.where(live > 0, 0.0, NEG)
    key = lax.broadcasted_iota(jnp.int32, (BLK, NEAR), 1)
    row = lax.broadcasted_iota(jnp.int32, (BLK, NEAR), 0)
    tri[...] = jnp.where((key < BLK) & (key > row), NEG, 0.0)

    theirs = kv.at[c, pl.ds(other, OWN)]
    wait_bytes(theirs, near_sem.at[2])
    remote(theirs, theirs, near_send_sem.at[3], near_sem.at[3], sibling).start()

    wait_bytes(far_send.at[pl.ds(0, DEV - 1)], far_sem)
    wait_bytes(mine, near_sem.at[1])
    wait_bytes(theirs, near_sem.at[3])

    near_slot = lax.shift_right_logical(lax.broadcasted_iota(jnp.int32, (1, NEAR), 1), 6)
    nt = (((1,), (1,)), ((), ()))
    nn = (((1,), (0,)), ((), ()))

    def step(t, carry):
        chip = lax.rem(z + t, CHIPS)
        wait_bytes(qb.at[pl.ds(2 * chip, 2)], q_sem.at[chip])
        rows = qb[pl.ds(2 * chip, 2)].reshape(2 * TOK, HD)
        far_keys = far[:, 0].reshape(FAR, HD)
        far_values = far[:, 1].reshape(FAR, HD)
        far_scores = lax.dot_general(rows, far_keys, nt, preferred_element_type=jnp.float32)
        far_scores = far_scores + far_bias[...]
        far_top = jnp.max(far_scores, 1, keepdims=True)
        tops, near_scores, near_values = [], [], []
        for b in range(4):
            block = 4 * chip + b
            keys, values = [], []
            bias = jnp.zeros((1, NEAR), jnp.float32)
            for s in range(SMAX):
                offset = so[me, s]
                target = jnp.maximum(block - offset, 0)
                their_chip = lax.shift_right_logical(target, 2)
                core = lax.shift_right_logical(target, 1) & 1
                place = (their_chip - 2 * g - 1) & (CHIPS - 1)
                half = target & 1
                keys.append(kv[core, place, 0, half])
                values.append(kv[core, place, 1, half])
                seen = (block >= offset) & (s < sc[me])
                bias = jnp.where(near_slot == s, jnp.where(seen, 0.0, NEG), bias)
            scores = lax.dot_general(
                rows[b * BLK : (b + 1) * BLK],
                jnp.concatenate(keys, 0),
                nt,
                preferred_element_type=jnp.float32,
            )
            scores = scores + (tri[...] + bias)
            near_scores.append(scores)
            near_values.append(jnp.concatenate(values, 0))
            tops.append(jnp.max(scores, 1, keepdims=True))
        top = jnp.maximum(far_top, jnp.concatenate(tops, 0)) * SCALE
        far_weights = jnp.exp2(far_scores * SCALE - top)
        total = jnp.sum(far_weights, 1, keepdims=True)
        mixed = lax.dot_general(
            far_weights.astype(jnp.bfloat16), far_values, nn, preferred_element_type=jnp.float32
        )
        for b in range(4):
            own = slice(b * BLK, (b + 1) * BLK)
            weights = jnp.exp2(near_scores[b] * SCALE - top[own])
            sums = total[own] + jnp.sum(weights, 1, keepdims=True)
            near_mixed = lax.dot_general(
                weights.astype(jnp.bfloat16),
                near_values[b],
                nn,
                preferred_element_type=jnp.float32,
            )
            done = (mixed[own] + near_mixed) / sums
            ob[2 * chip + b // 2, pl.ds((b % 2) * BLK, BLK), :] = done.astype(jnp.bfloat16)
        for core in range(2):
            device = 2 * chip + core

            @pl.when(device == me)
            def _():
                pltpu.make_async_copy(ob.at[device], out.at[:, columns(me)], out_sem).start()

            @pl.when(device != me)
            def _():
                remote(
                    ob.at[device], out.at[:, columns(me)], out_send_sem, out_sem, device
                ).start()

        return carry

    lax.fori_loop(0, CHIPS, step, 0)

    wait_bytes(ob, out_sem)
    most = ob.at[pl.ds(0, DEV - 1)]
    wait_bytes(most, out_send_sem)
    wait_bytes(most, q_send_sem)
    wait_bytes(far_send.at[pl.ds(0, DEV - 1)], far_send_sem)
    wait_bytes(kv.at[0, pl.ds(0, KVH - 1)], near_send_sem.at[0])
    wait_bytes(mine, near_send_sem.at[1])
    wait_bytes(mine, near_send_sem.at[2])
    wait_bytes(theirs, near_send_sem.at[3])


def shards(q, k, v, pk, pv, vb, vc, so, sc):
    hbm = pl.BlockSpec(memory_space=pl.ANY)
    smem = pl.BlockSpec(memory_space=pltpu.SMEM)
    dma = pltpu.SemaphoreType.DMA
    bf16 = jnp.bfloat16
    return pl.pallas_call(
        kernel,
        out_shape=jax.ShapeDtypeStruct((TOK, H * HD), bf16),
        in_specs=[hbm] * 5 + [smem] * 4,
        out_specs=hbm,
        scratch_shapes=[
            pltpu.VMEM((2, CHIPS, 2, 2, BLK, HD), bf16),
            pltpu.VMEM((DEV, 2, BLK, HD), bf16),
            pltpu.VMEM((DEV, 2, BLK, HD), bf16),
            pltpu.VMEM((OWN, BLK, KVH * HD), bf16),
            pltpu.VMEM((OWN, BLK, KVH * HD), bf16),
            pltpu.VMEM((DEV, TOK, HD), bf16),
            pltpu.VMEM((DEV, TOK, HD), bf16),
            pltpu.VMEM((1, FAR), jnp.float32),
            pltpu.VMEM((BLK, NEAR), jnp.float32),
            dma((4,)),
            dma((4,)),
            dma((4,)),
            dma,
            dma,
            dma((CHIPS,)),
            dma,
            dma,
            dma,
        ],
        compiler_params=pltpu.CompilerParams(
            collective_id=0, has_side_effects=True, vmem_limit_bytes=48 << 20
        ),
    )(
        q,
        k.reshape(2, BLK, KVH * HD),
        v.reshape(2, BLK, KVH * HD),
        pk.reshape(OWN, BLK, KVH * HD),
        pv.reshape(OWN, BLK, KVH * HD),
        vb,
        vc,
        so,
        sc,
    )


def solution(mesh):
    tokens = P(("req", "head"), None)
    return jax.shard_map(
        shards,
        mesh=mesh,
        in_specs=(tokens,) * 5 + (P("req", None), P("req"), P("req", None), P("req")),
        out_specs=tokens,
        check_vma=False,
    )
```

```python
import math

import jax
import jax.numpy as jnp
from jax import lax
from jax.experimental import pallas as pl
from jax.experimental.pallas import tpu as pltpu
from jax.sharding import PartitionSpec as P

H = 32
KVH = 8
HD = 128
BLK = 64
SMAX = 8
DEV = 32
CHIPS = 16
OWN = 8
TOK = 128
FAR = DEV * BLK
NEAR = SMAX * BLK
MESH = pl.DeviceIdType.MESH
SCALE = math.log2(math.e) / math.sqrt(HD)
NEG = -math.inf


def kernel(
    q,
    k,
    v,
    pk,
    pv,
    vb_hbm,
    vc_hbm,
    so_hbm,
    sc_hbm,
    out,
    kv,
    far,
    far_send,
    pkb,
    pvb,
    qb,
    ob,
    far_bias,
    tri,
    vb,
    vc,
    so,
    sc,
    load_sem,
    near_sem,
    near_send_sem,
    far_sem,
    far_send_sem,
    q_sem,
    q_send_sem,
    out_sem,
    out_send_sem,
):
    me = lax.axis_index("head")
    z, c = lax.div(me, 2), lax.rem(me, 2)
    g, odd = lax.div(z, 2), lax.rem(z, 2)
    sibling = 2 * z + 1 - c
    across = 2 * (2 * g + 1 - odd) + c

    def columns(index):
        return pl.ds(pl.multiple_of(index * HD, HD), HD)

    def remote(src, dst, send_sem, recv_sem, device):
        return pltpu.make_async_remote_copy(
            src_ref=src,
            dst_ref=dst,
            send_sem=send_sem,
            recv_sem=recv_sem,
            device_id={"head": device},
            device_id_type=MESH,
        )

    def wait_bytes(ref, sem):
        pltpu.make_async_copy(ref, ref, sem).wait()

    def turn(t):
        return jnp.where(lax.rem(t, 2) == 1, 8 - lax.div(t + 1, 2), lax.div(t, 2) - 8)

    def signal(semaphore, device):
        pl.semaphore_signal(semaphore, inc=1, device_id={"head": device}, device_id_type=MESH)

    right = lax.rem(z + 1, CHIPS)
    left = lax.rem(z + CHIPS - 1, CHIPS)
    barrier = pltpu.get_barrier_semaphore()

    def greet(t, carry):
        chip = lax.rem(z + turn(t) + CHIPS, CHIPS)
        for core in range(2):

            @pl.when(2 * chip + core != me)
            def _():
                signal(barrier, 2 * chip + core)

        return carry

    lax.fori_loop(0, CHIPS, greet, 0)
    metas = [
        pltpu.make_async_copy(source, target, load_sem.at[4 + i])
        for i, (source, target) in enumerate(
            ((vb_hbm, vb), (vc_hbm, vc), (so_hbm, so), (sc_hbm, sc))
        )
    ]
    for copy in metas:
        copy.start()
    load_k = pltpu.make_async_copy(pk, pkb, load_sem.at[0])
    load_v = pltpu.make_async_copy(pv, pvb, load_sem.at[1])
    load_k.start()
    load_v.start()

    spot = 15 * (1 - odd)
    own_k = pltpu.make_async_copy(k.at[:, :, columns(g)], kv.at[c, spot, 0], load_sem.at[2])
    own_v = pltpu.make_async_copy(v.at[:, :, columns(g)], kv.at[c, spot, 1], load_sem.at[3])
    own_k.start()
    own_v.start()
    pltpu.make_async_copy(q.at[:, columns(me)], qb.at[me], q_sem.at[z]).start()

    def near_out(chip):
        group = lax.div(chip, 2)
        place = lax.rem(z - 2 * group - 1 + 2 * CHIPS, CHIPS)
        for part, source in enumerate((k, v)):
            remote(
                source.at[:, :, columns(group)],
                kv.at[c, place, part],
                near_send_sem.at[0],
                near_sem.at[0],
                2 * chip + c,
            ).start()

    def picked(head):
        block = jnp.int32(0)
        count = vc[head]
        for t in range(DEV):
            entry = vb[head, t]
            mine = (lax.shift_right_logical(entry, 3) == me) & (t < count)
            block = block + jnp.where(mine, entry - OWN * me, 0)
        return block

    def pick(head, buffer, slot):
        block = picked(head)
        cols = columns(lax.div(head, H // KVH))
        buffer[slot, 0] = pkb[block, :, cols]
        buffer[slot, 1] = pvb[block, :, cols]

    def far_out(head):
        pick(head, far_send, head)
        remote(far_send.at[head], far.at[me], far_send_sem, far_sem, head).start()

    for copy in metas:
        copy.wait()
    load_k.wait()
    load_v.wait()
    pl.semaphore_wait(barrier, DEV - 1)

    def near_step(j, carry):
        ahead = lax.rem(z + j, CHIPS)
        behind = lax.rem(z - j + CHIPS, CHIPS)

        @pl.when(lax.rem(ahead, 2) == 0)
        def _():
            near_out(ahead)

        @pl.when(lax.rem(behind, 2) == 1)
        def _():
            near_out(behind)

        return carry

    lax.fori_loop(1, KVH, near_step, 0)

    def far_step(t, carry):
        chip = lax.rem(z + turn(t) + CHIPS, CHIPS)
        for core in range(2):

            @pl.when(2 * chip + core != me)
            def _():
                far_out(2 * chip + core)

        return carry

    lax.fori_loop(0, CHIPS, far_step, 0)
    pick(me, far, me)

    own_k.wait()
    own_v.wait()
    first = OWN * (1 - odd)
    other = OWN * odd
    mine = kv.at[c, pl.ds(first, OWN)]
    wait_bytes(kv.at[c, pl.ds(first, OWN - 1)], near_sem.at[0])
    remote(mine, mine, near_send_sem.at[1], near_sem.at[1], sibling).start()
    remote(mine, mine, near_send_sem.at[2], near_sem.at[2], across).start()

    def q_out(t, carry):
        chip = lax.rem(z - turn(t) + CHIPS, CHIPS)
        for core in range(2):
            device = 2 * chip + core

            @pl.when(device != me)
            def _():
                remote(
                    q.at[:, columns(device)], qb.at[me], q_send_sem, q_sem.at[z], device
                ).start()

        return carry

    lax.fori_loop(0, 16, q_out, 0)

    count = vc[me]
    lane = lax.broadcasted_iota(jnp.int32, (1, FAR), 1)
    slot = lax.shift_right_logical(lane, 6)
    live = jnp.zeros((1, FAR), jnp.int32)
    for t in range(DEV):
        owner = jnp.where(t < count, lax.shift_right_logical(vb[me, t], 3), -1)
        live = jnp.where(slot == owner, 1, live)
    far_bias[...] = jnp.where(live > 0, 0.0, NEG)
    key = lax.broadcasted_iota(jnp.int32, (BLK, NEAR), 1)
    row = lax.broadcasted_iota(jnp.int32, (BLK, NEAR), 0)
    tri[...] = jnp.where((key < BLK) & (key > row), NEG, 0.0)

    theirs = kv.at[c, pl.ds(other, OWN)]
    wait_bytes(theirs, near_sem.at[2])
    remote(theirs, theirs, near_send_sem.at[3], near_sem.at[3], sibling).start()

    wait_bytes(far_send.at[pl.ds(0, DEV - 1)], far_sem)
    wait_bytes(mine, near_sem.at[1])
    wait_bytes(theirs, near_sem.at[3])

    near_slot = lax.shift_right_logical(lax.broadcasted_iota(jnp.int32, (1, NEAR), 1), 6)
    nt = (((1,), (1,)), ((), ()))
    nn = (((1,), (0,)), ((), ()))

    def step(t, carry):
        chip = lax.rem(z + turn(t) + CHIPS, CHIPS)
        wait_bytes(qb.at[pl.ds(2 * chip, 2)], q_sem.at[chip])
        rows = qb[pl.ds(2 * chip, 2)].reshape(2 * TOK, HD)
        far_keys = far[:, 0].reshape(FAR, HD)
        far_values = far[:, 1].reshape(FAR, HD)
        far_scores = lax.dot_general(rows, far_keys, nt, preferred_element_type=jnp.float32)
        far_scores = far_scores + far_bias[...]
        far_top = jnp.max(far_scores, 1, keepdims=True)
        tops, near_scores, near_values = [], [], []
        for b in range(4):
            block = 4 * chip + b
            keys, values = [], []
            bias = jnp.zeros((1, NEAR), jnp.float32)
            for s in range(SMAX):
                offset = so[s, me]
                target = jnp.maximum(block - offset, 0)
                their_chip = lax.shift_right_logical(target, 2)
                core = lax.shift_right_logical(target, 1) & 1
                place = (their_chip - 2 * g - 1) & (CHIPS - 1)
                half = target & 1
                keys.append(kv[core, place, 0, half])
                values.append(kv[core, place, 1, half])
                seen = (block >= offset) & (s < sc[me])
                bias = jnp.where(near_slot == s, jnp.where(seen, 0.0, NEG), bias)
            scores = lax.dot_general(
                rows[b * BLK : (b + 1) * BLK],
                jnp.concatenate(keys, 0),
                nt,
                preferred_element_type=jnp.float32,
            )
            scores = scores + (tri[...] + bias)
            near_scores.append(scores)
            near_values.append(jnp.concatenate(values, 0))
            tops.append(jnp.max(scores, 1, keepdims=True))
        top = jnp.maximum(far_top, jnp.concatenate(tops, 0)) * SCALE
        far_weights = jnp.exp2(far_scores * SCALE - top)
        total = jnp.sum(far_weights, 1, keepdims=True)
        mixed = lax.dot_general(
            far_weights.astype(jnp.bfloat16), far_values, nn, preferred_element_type=jnp.float32
        )
        for b in range(4):
            own = slice(b * BLK, (b + 1) * BLK)
            weights = jnp.exp2(near_scores[b] * SCALE - top[own])
            sums = total[own] + jnp.sum(weights, 1, keepdims=True)
            near_mixed = lax.dot_general(
                weights.astype(jnp.bfloat16),
                near_values[b],
                nn,
                preferred_element_type=jnp.float32,
            )
            done = (mixed[own] + near_mixed) / sums
            ob[2 * chip + b // 2, pl.ds((b % 2) * BLK, BLK), :] = done.astype(jnp.bfloat16)
        for core in range(2):
            device = 2 * chip + core

            @pl.when(device == me)
            def _():
                pltpu.make_async_copy(ob.at[device], out.at[:, columns(me)], out_sem).start()

            @pl.when(device != me)
            def _():
                remote(
                    ob.at[device], out.at[:, columns(me)], out_send_sem, out_sem, device
                ).start()

        return carry

    lax.fori_loop(0, CHIPS, step, 0)

    wait_bytes(ob, out_sem)
    most = ob.at[pl.ds(0, DEV - 1)]
    wait_bytes(most, out_send_sem)
    wait_bytes(most, q_send_sem)
    wait_bytes(far_send.at[pl.ds(0, DEV - 1)], far_send_sem)
    wait_bytes(kv.at[0, pl.ds(0, KVH - 1)], near_send_sem.at[0])
    wait_bytes(mine, near_send_sem.at[1])
    wait_bytes(mine, near_send_sem.at[2])
    wait_bytes(theirs, near_send_sem.at[3])


def shards(q, k, v, pk, pv, vb, vc, so, sc):
    hbm = pl.BlockSpec(memory_space=pl.ANY)
    dma = pltpu.SemaphoreType.DMA
    bf16 = jnp.bfloat16
    return pl.pallas_call(
        kernel,
        out_shape=jax.ShapeDtypeStruct((TOK, H * HD), bf16),
        in_specs=[hbm] * 9,
        out_specs=hbm,
        scratch_shapes=[
            pltpu.VMEM((2, CHIPS, 2, 2, BLK, HD), bf16),
            pltpu.VMEM((DEV, 2, BLK, HD), bf16),
            pltpu.VMEM((DEV, 2, BLK, HD), bf16),
            pltpu.VMEM((OWN, BLK, KVH * HD), bf16),
            pltpu.VMEM((OWN, BLK, KVH * HD), bf16),
            pltpu.VMEM((DEV, TOK, HD), bf16),
            pltpu.VMEM((DEV, TOK, HD), bf16),
            pltpu.VMEM((1, FAR), jnp.float32),
            pltpu.VMEM((BLK, NEAR), jnp.float32),
            pltpu.SMEM((DEV, DEV), jnp.int32),
            pltpu.SMEM((DEV,), jnp.int32),
            pltpu.SMEM((SMAX, DEV), jnp.int32),
            pltpu.SMEM((DEV,), jnp.int32),
            dma((8,)),
            dma((4,)),
            dma((4,)),
            dma,
            dma,
            dma((CHIPS,)),
            dma,
            dma,
            dma,
        ],
        compiler_params=pltpu.CompilerParams(
            collective_id=0, has_side_effects=True, vmem_limit_bytes=60 << 20
        ),
    )(
        q,
        k.reshape(2, BLK, KVH * HD),
        v.reshape(2, BLK, KVH * HD),
        pk.reshape(OWN, BLK, KVH * HD),
        pv.reshape(OWN, BLK, KVH * HD),
        vb,
        vc,
        so.T,
        sc,
    )


def solution(mesh):
    tokens = P(("req", "head"), None)
    return jax.shard_map(
        shards,
        mesh=mesh,
        in_specs=(tokens,) * 5 + (P("req", None), P("req"), P("req", None), P("req")),
        out_specs=tokens,
        check_vma=False,
    )
```

```python
import math

import jax
import jax.numpy as jnp
from jax import lax
from jax.experimental import pallas as pl
from jax.experimental.pallas import tpu as pltpu
from jax.sharding import PartitionSpec as P

H = 32
KVH = 8
HD = 128
BLK = 64
SMAX = 8
DEV = 32
CHIPS = 16
OWN = 8
TOK = 128
FAR = DEV * BLK
NEAR = SMAX * BLK
RADIUS = 2
MESH = pl.DeviceIdType.MESH
SCALE = math.log2(math.e) / math.sqrt(HD)
NEG = -math.inf


def kernel(
    q,
    k,
    v,
    pk,
    pv,
    vb_hbm,
    vc_hbm,
    so_hbm,
    sc_hbm,
    out,
    kv,
    far,
    far_send,
    pkb,
    pvb,
    qb,
    ob,
    far_bias,
    tri,
    vb,
    vc,
    so,
    sc,
    load_sem,
    near_sem,
    near_send_sem,
    far_sem,
    far_send_sem,
    q_sem,
    q_send_sem,
    out_sem,
    out_send_sem,
    known_sem,
):
    me = lax.axis_index("head")
    z, c = lax.div(me, 2), lax.rem(me, 2)
    g, odd = lax.div(z, 2), lax.rem(z, 2)
    sibling = 2 * z + 1 - c
    across = 2 * (2 * g + 1 - odd) + c

    def columns(index):
        return pl.ds(pl.multiple_of(index * HD, HD), HD)

    def remote(src, dst, send_sem, recv_sem, device):
        return pltpu.make_async_remote_copy(
            src_ref=src,
            dst_ref=dst,
            send_sem=send_sem,
            recv_sem=recv_sem,
            device_id={"head": device},
            device_id_type=MESH,
        )

    def wait_bytes(ref, sem):
        pltpu.make_async_copy(ref, ref, sem).wait()

    def turn(t):
        return jnp.where(lax.rem(t, 2) == 1, 8 - lax.div(t + 1, 2), lax.div(t, 2) - 8)

    def signal(semaphore, device):
        pl.semaphore_signal(semaphore, inc=1, device_id={"head": device}, device_id_type=MESH)

    barrier = pltpu.get_barrier_semaphore()
    signal(barrier, sibling)
    for distance in range(1, RADIUS + 1):
        for chip in (lax.rem(z + distance, CHIPS), lax.rem(z + CHIPS - distance, CHIPS)):
            for core in range(2):
                signal(barrier, 2 * chip + core)
    metas = [
        pltpu.make_async_copy(source, target, load_sem.at[4 + i])
        for i, (source, target) in enumerate(
            ((vb_hbm, vb), (vc_hbm, vc), (so_hbm, so), (sc_hbm, sc))
        )
    ]
    for copy in metas:
        copy.start()
    load_k = pltpu.make_async_copy(pk, pkb, load_sem.at[0])
    load_v = pltpu.make_async_copy(pv, pvb, load_sem.at[1])
    load_k.start()
    load_v.start()

    spot = 15 * (1 - odd)
    own_k = pltpu.make_async_copy(k.at[:, :, columns(g)], kv.at[c, spot, 0], load_sem.at[2])
    own_v = pltpu.make_async_copy(v.at[:, :, columns(g)], kv.at[c, spot, 1], load_sem.at[3])
    own_k.start()
    own_v.start()
    pltpu.make_async_copy(q.at[:, columns(me)], qb.at[me], q_sem.at[z]).start()

    def near_out(chip):
        group = lax.div(chip, 2)
        place = lax.rem(z - 2 * group - 1 + 2 * CHIPS, CHIPS)
        for part, source in enumerate((k, v)):
            remote(
                source.at[:, :, columns(group)],
                kv.at[c, place, part],
                near_send_sem.at[0],
                near_sem.at[0],
                2 * chip + c,
            ).start()

    def picked(head):
        block = jnp.int32(0)
        count = vc[head]
        for t in range(DEV):
            entry = vb[head, t]
            mine = (lax.shift_right_logical(entry, 3) == me) & (t < count)
            block = block + jnp.where(mine, entry - OWN * me, 0)
        return block

    def pick(head, buffer, slot):
        block = picked(head)
        cols = columns(lax.div(head, H // KVH))
        buffer[slot, 0] = pkb[block, :, cols]
        buffer[slot, 1] = pvb[block, :, cols]

    def far_out(head):
        pick(head, far_send, head)
        remote(far_send.at[head], far.at[me], far_send_sem, far_sem, head).start()

    for copy in metas:
        copy.wait()
    load_k.wait()
    load_v.wait()
    pl.semaphore_wait(barrier, 4 * RADIUS + 1)

    def serve(distance, carry):
        ahead = lax.rem(z + distance, CHIPS)
        behind = lax.rem(z + CHIPS - distance, CHIPS)

        @pl.when(lax.rem(ahead, 2) == 0)
        def _():
            near_out(ahead)

        @pl.when(lax.rem(behind, 2) == 1)
        def _():
            near_out(behind)

        return carry

    done, reach, rounds = 0, RADIUS, 0
    while reach < CHIPS // 2:
        for chip in (lax.rem(z + reach, CHIPS), lax.rem(z + CHIPS - reach, CHIPS)):
            signal(known_sem.at[rounds], 2 * chip + c)
        lax.fori_loop(done + 1, reach + 1, serve, 0)
        pl.semaphore_wait(known_sem.at[rounds], 2)
        done, reach, rounds = reach, 2 * reach, rounds + 1
    lax.fori_loop(done + 1, CHIPS // 2, serve, 0)

    def far_step(t, carry):
        chip = lax.rem(z + turn(t) + CHIPS, CHIPS)
        for core in range(2):

            @pl.when(2 * chip + core != me)
            def _():
                far_out(2 * chip + core)

        return carry

    lax.fori_loop(0, CHIPS, far_step, 0)
    pick(me, far, me)

    own_k.wait()
    own_v.wait()
    first = OWN * (1 - odd)
    other = OWN * odd
    mine = kv.at[c, pl.ds(first, OWN)]
    wait_bytes(kv.at[c, pl.ds(first, OWN - 1)], near_sem.at[0])
    remote(mine, mine, near_send_sem.at[1], near_sem.at[1], sibling).start()
    remote(mine, mine, near_send_sem.at[2], near_sem.at[2], across).start()

    def q_out(t, carry):
        chip = lax.rem(z - turn(t) + CHIPS, CHIPS)
        for core in range(2):
            device = 2 * chip + core

            @pl.when(device != me)
            def _():
                remote(
                    q.at[:, columns(device)], qb.at[me], q_send_sem, q_sem.at[z], device
                ).start()

        return carry

    lax.fori_loop(0, 16, q_out, 0)

    count = vc[me]
    lane = lax.broadcasted_iota(jnp.int32, (1, FAR), 1)
    slot = lax.shift_right_logical(lane, 6)
    live = jnp.zeros((1, FAR), jnp.int32)
    for t in range(DEV):
        owner = jnp.where(t < count, lax.shift_right_logical(vb[me, t], 3), -1)
        live = jnp.where(slot == owner, 1, live)
    far_bias[...] = jnp.where(live > 0, 0.0, NEG)
    key = lax.broadcasted_iota(jnp.int32, (BLK, NEAR), 1)
    row = lax.broadcasted_iota(jnp.int32, (BLK, NEAR), 0)
    tri[...] = jnp.where((key < BLK) & (key > row), NEG, 0.0)

    theirs = kv.at[c, pl.ds(other, OWN)]
    wait_bytes(theirs, near_sem.at[2])
    remote(theirs, theirs, near_send_sem.at[3], near_sem.at[3], sibling).start()

    wait_bytes(far_send.at[pl.ds(0, DEV - 1)], far_sem)
    wait_bytes(mine, near_sem.at[1])
    wait_bytes(theirs, near_sem.at[3])

    near_slot = lax.shift_right_logical(lax.broadcasted_iota(jnp.int32, (1, NEAR), 1), 6)
    nt = (((1,), (1,)), ((), ()))
    nn = (((1,), (0,)), ((), ()))

    def step(t, carry):
        chip = lax.rem(z + turn(t) + CHIPS, CHIPS)
        wait_bytes(qb.at[pl.ds(2 * chip, 2)], q_sem.at[chip])
        rows = qb[pl.ds(2 * chip, 2)].reshape(2 * TOK, HD)
        far_keys = far[:, 0].reshape(FAR, HD)
        far_values = far[:, 1].reshape(FAR, HD)
        far_scores = lax.dot_general(rows, far_keys, nt, preferred_element_type=jnp.float32)
        far_scores = far_scores + far_bias[...]
        far_top = jnp.max(far_scores, 1, keepdims=True)
        tops, near_scores, near_values = [], [], []
        for b in range(4):
            block = 4 * chip + b
            keys, values = [], []
            bias = jnp.zeros((1, NEAR), jnp.float32)
            for s in range(SMAX):
                offset = so[s, me]
                target = jnp.maximum(block - offset, 0)
                their_chip = lax.shift_right_logical(target, 2)
                core = lax.shift_right_logical(target, 1) & 1
                place = (their_chip - 2 * g - 1) & (CHIPS - 1)
                half = target & 1
                keys.append(kv[core, place, 0, half])
                values.append(kv[core, place, 1, half])
                seen = (block >= offset) & (s < sc[me])
                bias = jnp.where(near_slot == s, jnp.where(seen, 0.0, NEG), bias)
            scores = lax.dot_general(
                rows[b * BLK : (b + 1) * BLK],
                jnp.concatenate(keys, 0),
                nt,
                preferred_element_type=jnp.float32,
            )
            scores = scores + (tri[...] + bias)
            near_scores.append(scores)
            near_values.append(jnp.concatenate(values, 0))
            tops.append(jnp.max(scores, 1, keepdims=True))
        top = jnp.maximum(far_top, jnp.concatenate(tops, 0)) * SCALE
        far_weights = jnp.exp2(far_scores * SCALE - top)
        total = jnp.sum(far_weights, 1, keepdims=True)
        mixed = lax.dot_general(
            far_weights.astype(jnp.bfloat16), far_values, nn, preferred_element_type=jnp.float32
        )
        for b in range(4):
            own = slice(b * BLK, (b + 1) * BLK)
            weights = jnp.exp2(near_scores[b] * SCALE - top[own])
            sums = total[own] + jnp.sum(weights, 1, keepdims=True)
            near_mixed = lax.dot_general(
                weights.astype(jnp.bfloat16),
                near_values[b],
                nn,
                preferred_element_type=jnp.float32,
            )
            done = (mixed[own] + near_mixed) / sums
            ob[2 * chip + b // 2, pl.ds((b % 2) * BLK, BLK), :] = done.astype(jnp.bfloat16)
        for core in range(2):
            device = 2 * chip + core

            @pl.when(device == me)
            def _():
                pltpu.make_async_copy(ob.at[device], out.at[:, columns(me)], out_sem).start()

            @pl.when(device != me)
            def _():
                remote(
                    ob.at[device], out.at[:, columns(me)], out_send_sem, out_sem, device
                ).start()

        return carry

    lax.fori_loop(0, CHIPS, step, 0)

    wait_bytes(ob, out_sem)
    most = ob.at[pl.ds(0, DEV - 1)]
    wait_bytes(most, out_send_sem)
    wait_bytes(most, q_send_sem)
    wait_bytes(far_send.at[pl.ds(0, DEV - 1)], far_send_sem)
    wait_bytes(kv.at[0, pl.ds(0, KVH - 1)], near_send_sem.at[0])
    wait_bytes(mine, near_send_sem.at[1])
    wait_bytes(mine, near_send_sem.at[2])
    wait_bytes(theirs, near_send_sem.at[3])


def shards(q, k, v, pk, pv, vb, vc, so, sc):
    hbm = pl.BlockSpec(memory_space=pl.ANY)
    dma = pltpu.SemaphoreType.DMA
    bf16 = jnp.bfloat16
    return pl.pallas_call(
        kernel,
        out_shape=jax.ShapeDtypeStruct((TOK, H * HD), bf16),
        in_specs=[hbm] * 9,
        out_specs=hbm,
        scratch_shapes=[
            pltpu.VMEM((2, CHIPS, 2, 2, BLK, HD), bf16),
            pltpu.VMEM((DEV, 2, BLK, HD), bf16),
            pltpu.VMEM((DEV, 2, BLK, HD), bf16),
            pltpu.VMEM((OWN, BLK, KVH * HD), bf16),
            pltpu.VMEM((OWN, BLK, KVH * HD), bf16),
            pltpu.VMEM((DEV, TOK, HD), bf16),
            pltpu.VMEM((DEV, TOK, HD), bf16),
            pltpu.VMEM((1, FAR), jnp.float32),
            pltpu.VMEM((BLK, NEAR), jnp.float32),
            pltpu.SMEM((DEV, DEV), jnp.int32),
            pltpu.SMEM((DEV,), jnp.int32),
            pltpu.SMEM((SMAX, DEV), jnp.int32),
            pltpu.SMEM((DEV,), jnp.int32),
            dma((8,)),
            dma((4,)),
            dma((4,)),
            dma,
            dma,
            dma((CHIPS,)),
            dma,
            dma,
            dma,
            pltpu.SemaphoreType.REGULAR((4,)),
        ],
        compiler_params=pltpu.CompilerParams(
            collective_id=0, has_side_effects=True, vmem_limit_bytes=60 << 20
        ),
    )(
        q,
        k.reshape(2, BLK, KVH * HD),
        v.reshape(2, BLK, KVH * HD),
        pk.reshape(OWN, BLK, KVH * HD),
        pv.reshape(OWN, BLK, KVH * HD),
        vb,
        vc,
        so.T,
        sc,
    )


def solution(mesh):
    tokens = P(("req", "head"), None)
    return jax.shard_map(
        shards,
        mesh=mesh,
        in_specs=(tokens,) * 5 + (P("req", None), P("req"), P("req", None), P("req")),
        out_specs=tokens,
        check_vma=False,
    )
```

```python
import math

import jax
import jax.numpy as jnp
from jax import lax
from jax.experimental import pallas as pl
from jax.experimental.pallas import tpu as pltpu
from jax.sharding import PartitionSpec as P

H = 32
KVH = 8
HD = 128
BLK = 64
SMAX = 8
DEV = 32
CHIPS = 16
OWN = 8
TOK = 128
FAR = DEV * BLK
NEAR = SMAX * BLK
RADIUS = 2
MESH = pl.DeviceIdType.MESH
SCALE = math.log2(math.e) / math.sqrt(HD)
NEG = -math.inf


def kernel(
    q,
    k,
    v,
    pk,
    pv,
    vb_hbm,
    vc_hbm,
    so_hbm,
    sc_hbm,
    out,
    kv,
    far,
    far_send,
    pkb,
    pvb,
    qb,
    ob,
    far_bias,
    tri,
    vb,
    vc,
    so,
    sc,
    load_sem,
    near_sem,
    near_send_sem,
    far_sem,
    far_send_sem,
    q_sem,
    q_send_sem,
    out_sem,
    out_send_sem,
    known_sem,
):
    me = lax.axis_index("head")
    z, c = lax.div(me, 2), lax.rem(me, 2)
    g, odd = lax.div(z, 2), lax.rem(z, 2)
    sibling = 2 * z + 1 - c
    across = 2 * (2 * g + 1 - odd) + c

    def columns(index):
        return pl.ds(pl.multiple_of(index * HD, HD), HD)

    def remote(src, dst, send_sem, recv_sem, device):
        return pltpu.make_async_remote_copy(
            src_ref=src,
            dst_ref=dst,
            send_sem=send_sem,
            recv_sem=recv_sem,
            device_id={"head": device},
            device_id_type=MESH,
        )

    def wait_bytes(ref, sem):
        pltpu.make_async_copy(ref, ref, sem).wait()

    def turn(t):
        return jnp.where(lax.rem(t, 2) == 1, 8 - lax.div(t + 1, 2), lax.div(t, 2) - 8)

    def mixed(t):
        pair = lax.div(t + 1, 2)
        distance = jnp.where(lax.rem(pair, 2) == 1, 8 - lax.div(pair + 1, 2), lax.div(pair, 2))
        distance = jnp.where(t == 0, 8, jnp.where(t == 15, 0, distance))
        return jnp.where(lax.rem(t, 2) == 1, distance, -distance)

    def signal(semaphore, device):
        pl.semaphore_signal(semaphore, inc=1, device_id={"head": device}, device_id_type=MESH)

    barrier = pltpu.get_barrier_semaphore()
    signal(barrier, sibling)
    for distance in range(1, RADIUS + 1):
        for chip in (lax.rem(z + distance, CHIPS), lax.rem(z + CHIPS - distance, CHIPS)):
            for core in range(2):
                signal(barrier, 2 * chip + core)
    metas = [
        pltpu.make_async_copy(source, target, load_sem.at[4 + i])
        for i, (source, target) in enumerate(
            ((vb_hbm, vb), (vc_hbm, vc), (so_hbm, so), (sc_hbm, sc))
        )
    ]
    for copy in metas:
        copy.start()
    load_k = pltpu.make_async_copy(pk, pkb, load_sem.at[0])
    load_v = pltpu.make_async_copy(pv, pvb, load_sem.at[1])
    load_k.start()
    load_v.start()

    spot = 15 * (1 - odd)
    own_k = pltpu.make_async_copy(k.at[:, :, columns(g)], kv.at[c, spot, 0], load_sem.at[2])
    own_v = pltpu.make_async_copy(v.at[:, :, columns(g)], kv.at[c, spot, 1], load_sem.at[3])
    own_k.start()
    own_v.start()
    pltpu.make_async_copy(q.at[:, columns(me)], qb.at[me], q_sem.at[z]).start()

    def near_out(chip):
        group = lax.div(chip, 2)
        place = lax.rem(z - 2 * group - 1 + 2 * CHIPS, CHIPS)
        for part, source in enumerate((k, v)):
            remote(
                source.at[:, :, columns(group)],
                kv.at[c, place, part],
                near_send_sem.at[0],
                near_sem.at[0],
                2 * chip + c,
            ).start()

    def picked(head):
        block = jnp.int32(0)
        count = vc[head]
        for t in range(DEV):
            entry = vb[head, t]
            mine = (lax.shift_right_logical(entry, 3) == me) & (t < count)
            block = block + jnp.where(mine, entry - OWN * me, 0)
        return block

    def pick(head, buffer, slot):
        block = picked(head)
        cols = columns(lax.div(head, H // KVH))
        buffer[slot, 0] = pkb[block, :, cols]
        buffer[slot, 1] = pvb[block, :, cols]

    def far_out(head):
        pick(head, far_send, head)
        remote(far_send.at[head], far.at[me], far_send_sem, far_sem, head).start()

    for copy in metas:
        copy.wait()
    load_k.wait()
    load_v.wait()
    pl.semaphore_wait(barrier, 4 * RADIUS + 1)

    def serve(distance, carry):
        ahead = lax.rem(z + distance, CHIPS)
        behind = lax.rem(z + CHIPS - distance, CHIPS)

        @pl.when(lax.rem(ahead, 2) == 0)
        def _():
            near_out(ahead)

        @pl.when(lax.rem(behind, 2) == 1)
        def _():
            near_out(behind)

        return carry

    done, reach, rounds = 0, RADIUS, 0
    while reach < CHIPS // 2:
        for chip in (lax.rem(z + reach, CHIPS), lax.rem(z + CHIPS - reach, CHIPS)):
            signal(known_sem.at[rounds], 2 * chip + c)
        lax.fori_loop(done + 1, reach + 1, serve, 0)
        pl.semaphore_wait(known_sem.at[rounds], 2)
        done, reach, rounds = reach, 2 * reach, rounds + 1
    lax.fori_loop(done + 1, CHIPS // 2, serve, 0)

    def far_step(t, carry):
        chip = lax.rem(z + mixed(t) + CHIPS, CHIPS)
        for core in range(2):

            @pl.when(2 * chip + core != me)
            def _():
                far_out(2 * chip + core)

        return carry

    lax.fori_loop(0, CHIPS, far_step, 0)
    pick(me, far, me)

    own_k.wait()
    own_v.wait()
    first = OWN * (1 - odd)
    other = OWN * odd
    mine = kv.at[c, pl.ds(first, OWN)]
    wait_bytes(kv.at[c, pl.ds(first, OWN - 1)], near_sem.at[0])
    remote(mine, mine, near_send_sem.at[1], near_sem.at[1], sibling).start()
    remote(mine, mine, near_send_sem.at[2], near_sem.at[2], across).start()

    def q_out(t, carry):
        chip = lax.rem(z - mixed(t) + CHIPS, CHIPS)
        for core in range(2):
            device = 2 * chip + core

            @pl.when(device != me)
            def _():
                remote(
                    q.at[:, columns(device)], qb.at[me], q_send_sem, q_sem.at[z], device
                ).start()

        return carry

    lax.fori_loop(0, 16, q_out, 0)

    count = vc[me]
    lane = lax.broadcasted_iota(jnp.int32, (1, FAR), 1)
    slot = lax.shift_right_logical(lane, 6)
    live = jnp.zeros((1, FAR), jnp.int32)
    for t in range(DEV):
        owner = jnp.where(t < count, lax.shift_right_logical(vb[me, t], 3), -1)
        live = jnp.where(slot == owner, 1, live)
    far_bias[...] = jnp.where(live > 0, 0.0, NEG)
    key = lax.broadcasted_iota(jnp.int32, (BLK, NEAR), 1)
    row = lax.broadcasted_iota(jnp.int32, (BLK, NEAR), 0)
    tri[...] = jnp.where((key < BLK) & (key > row), NEG, 0.0)

    theirs = kv.at[c, pl.ds(other, OWN)]
    wait_bytes(theirs, near_sem.at[2])
    remote(theirs, theirs, near_send_sem.at[3], near_sem.at[3], sibling).start()

    wait_bytes(far_send.at[pl.ds(0, DEV - 1)], far_sem)
    wait_bytes(mine, near_sem.at[1])
    wait_bytes(theirs, near_sem.at[3])

    near_slot = lax.shift_right_logical(lax.broadcasted_iota(jnp.int32, (1, NEAR), 1), 6)
    nt = (((1,), (1,)), ((), ()))
    nn = (((1,), (0,)), ((), ()))

    def step(t, carry):
        chip = lax.rem(z + turn(t) + CHIPS, CHIPS)
        wait_bytes(qb.at[pl.ds(2 * chip, 2)], q_sem.at[chip])
        rows = qb[pl.ds(2 * chip, 2)].reshape(2 * TOK, HD)
        far_keys = far[:, 0].reshape(FAR, HD)
        far_values = far[:, 1].reshape(FAR, HD)
        far_scores = lax.dot_general(rows, far_keys, nt, preferred_element_type=jnp.float32)
        far_scores = far_scores + far_bias[...]
        far_top = jnp.max(far_scores, 1, keepdims=True)
        tops, near_scores, near_values = [], [], []
        for b in range(4):
            block = 4 * chip + b
            keys, values = [], []
            bias = jnp.zeros((1, NEAR), jnp.float32)
            for s in range(SMAX):
                offset = so[s, me]
                target = jnp.maximum(block - offset, 0)
                their_chip = lax.shift_right_logical(target, 2)
                core = lax.shift_right_logical(target, 1) & 1
                place = (their_chip - 2 * g - 1) & (CHIPS - 1)
                half = target & 1
                keys.append(kv[core, place, 0, half])
                values.append(kv[core, place, 1, half])
                seen = (block >= offset) & (s < sc[me])
                bias = jnp.where(near_slot == s, jnp.where(seen, 0.0, NEG), bias)
            scores = lax.dot_general(
                rows[b * BLK : (b + 1) * BLK],
                jnp.concatenate(keys, 0),
                nt,
                preferred_element_type=jnp.float32,
            )
            scores = scores + (tri[...] + bias)
            near_scores.append(scores)
            near_values.append(jnp.concatenate(values, 0))
            tops.append(jnp.max(scores, 1, keepdims=True))
        top = jnp.maximum(far_top, jnp.concatenate(tops, 0)) * SCALE
        far_weights = jnp.exp2(far_scores * SCALE - top)
        total = jnp.sum(far_weights, 1, keepdims=True)
        mixed = lax.dot_general(
            far_weights.astype(jnp.bfloat16), far_values, nn, preferred_element_type=jnp.float32
        )
        for b in range(4):
            own = slice(b * BLK, (b + 1) * BLK)
            weights = jnp.exp2(near_scores[b] * SCALE - top[own])
            sums = total[own] + jnp.sum(weights, 1, keepdims=True)
            near_mixed = lax.dot_general(
                weights.astype(jnp.bfloat16),
                near_values[b],
                nn,
                preferred_element_type=jnp.float32,
            )
            done = (mixed[own] + near_mixed) / sums
            ob[2 * chip + b // 2, pl.ds((b % 2) * BLK, BLK), :] = done.astype(jnp.bfloat16)
        for core in range(2):
            device = 2 * chip + core

            @pl.when(device == me)
            def _():
                pltpu.make_async_copy(ob.at[device], out.at[:, columns(me)], out_sem).start()

            @pl.when(device != me)
            def _():
                remote(
                    ob.at[device], out.at[:, columns(me)], out_send_sem, out_sem, device
                ).start()

        return carry

    lax.fori_loop(0, CHIPS, step, 0)

    wait_bytes(ob, out_sem)
    most = ob.at[pl.ds(0, DEV - 1)]
    wait_bytes(most, out_send_sem)
    wait_bytes(most, q_send_sem)
    wait_bytes(far_send.at[pl.ds(0, DEV - 1)], far_send_sem)
    wait_bytes(kv.at[0, pl.ds(0, KVH - 1)], near_send_sem.at[0])
    wait_bytes(mine, near_send_sem.at[1])
    wait_bytes(mine, near_send_sem.at[2])
    wait_bytes(theirs, near_send_sem.at[3])


def shards(q, k, v, pk, pv, vb, vc, so, sc):
    hbm = pl.BlockSpec(memory_space=pl.ANY)
    dma = pltpu.SemaphoreType.DMA
    bf16 = jnp.bfloat16
    return pl.pallas_call(
        kernel,
        out_shape=pltpu.VMEM((TOK, H * HD), bf16),
        in_specs=[hbm] * 9,
        out_specs=pl.BlockSpec(memory_space=pltpu.VMEM),
        scratch_shapes=[
            pltpu.VMEM((2, CHIPS, 2, 2, BLK, HD), bf16),
            pltpu.VMEM((DEV, 2, BLK, HD), bf16),
            pltpu.VMEM((DEV, 2, BLK, HD), bf16),
            pltpu.VMEM((OWN, BLK, KVH * HD), bf16),
            pltpu.VMEM((OWN, BLK, KVH * HD), bf16),
            pltpu.VMEM((DEV, TOK, HD), bf16),
            pltpu.VMEM((DEV, TOK, HD), bf16),
            pltpu.VMEM((1, FAR), jnp.float32),
            pltpu.VMEM((BLK, NEAR), jnp.float32),
            pltpu.SMEM((DEV, DEV), jnp.int32),
            pltpu.SMEM((DEV,), jnp.int32),
            pltpu.SMEM((SMAX, DEV), jnp.int32),
            pltpu.SMEM((DEV,), jnp.int32),
            dma((8,)),
            dma((4,)),
            dma((4,)),
            dma,
            dma,
            dma((CHIPS,)),
            dma,
            dma,
            dma,
            pltpu.SemaphoreType.REGULAR((4,)),
        ],
        compiler_params=pltpu.CompilerParams(
            collective_id=0, has_side_effects=True, vmem_limit_bytes=60 << 20
        ),
    )(
        q,
        k.reshape(2, BLK, KVH * HD),
        v.reshape(2, BLK, KVH * HD),
        pk.reshape(OWN, BLK, KVH * HD),
        pv.reshape(OWN, BLK, KVH * HD),
        vb,
        vc,
        so.T,
        sc,
    )


def solution(mesh):
    tokens = P(("req", "head"), None)
    return jax.shard_map(
        shards,
        mesh=mesh,
        in_specs=(tokens,) * 5 + (P("req", None), P("req"), P("req", None), P("req")),
        out_specs=tokens,
        check_vma=False,
    )
```

```python
import math

import jax
import jax.numpy as jnp
from jax import lax
from jax.experimental import pallas as pl
from jax.experimental.pallas import tpu as pltpu
from jax.sharding import PartitionSpec as P

H = 32
KVH = 8
HD = 128
BLK = 64
SMAX = 8
DEV = 32
CHIPS = 16
OWN = 8
TOK = 128
FAR = DEV * BLK
NEAR = SMAX * BLK
RADIUS = 2
MESH = pl.DeviceIdType.MESH
SCALE = math.log2(math.e) / math.sqrt(HD)
NEG = -math.inf


def kernel(
    q,
    k,
    v,
    pk,
    pv,
    vb_hbm,
    vc_hbm,
    so_hbm,
    sc_hbm,
    out,
    kv,
    far,
    far_send,
    pkb,
    pvb,
    qb,
    ob,
    far_bias,
    tri,
    vb,
    vc,
    so,
    sc,
    load_sem,
    near_sem,
    near_send_sem,
    far_sem,
    far_send_sem,
    q_sem,
    q_send_sem,
    out_sem,
    out_send_sem,
    known_sem,
):
    me = lax.axis_index("head")
    z, c = lax.div(me, 2), lax.rem(me, 2)
    g, odd = lax.div(z, 2), lax.rem(z, 2)
    sibling = 2 * z + 1 - c
    across = 2 * (2 * g + 1 - odd) + c

    def columns(index):
        return pl.ds(pl.multiple_of(index * HD, HD), HD)

    def remote(src, dst, send_sem, recv_sem, device):
        return pltpu.make_async_remote_copy(
            src_ref=src,
            dst_ref=dst,
            send_sem=send_sem,
            recv_sem=recv_sem,
            device_id={"head": device},
            device_id_type=MESH,
        )

    def wait_bytes(ref, sem):
        pltpu.make_async_copy(ref, ref, sem).wait()

    def turn(t):
        return jnp.where(lax.rem(t, 2) == 1, 8 - lax.div(t + 1, 2), lax.div(t, 2) - 8)

    def mixed(t):
        pair = lax.div(t + 1, 2)
        distance = jnp.where(lax.rem(pair, 2) == 1, 8 - lax.div(pair + 1, 2), lax.div(pair, 2))
        distance = jnp.where(t == 0, 8, jnp.where(t == 15, 0, distance))
        return jnp.where(lax.rem(t, 2) == 1, distance, -distance)

    def signal(semaphore, device):
        pl.semaphore_signal(semaphore, inc=1, device_id={"head": device}, device_id_type=MESH)

    barrier = pltpu.get_barrier_semaphore()
    signal(barrier, sibling)
    for distance in range(1, RADIUS + 1):
        for chip in (lax.rem(z + distance, CHIPS), lax.rem(z + CHIPS - distance, CHIPS)):
            for core in range(2):
                signal(barrier, 2 * chip + core)
    metas = [
        pltpu.make_async_copy(source, target, load_sem.at[4 + i])
        for i, (source, target) in enumerate(
            ((vb_hbm, vb), (vc_hbm, vc), (so_hbm, so), (sc_hbm, sc))
        )
    ]
    for copy in metas:
        copy.start()
    load_k = pltpu.make_async_copy(pk, pkb, load_sem.at[0])
    load_v = pltpu.make_async_copy(pv, pvb, load_sem.at[1])
    load_k.start()
    load_v.start()

    spot = 15 * (1 - odd)
    own_k = pltpu.make_async_copy(k.at[:, :, columns(g)], kv.at[c, spot, 0], load_sem.at[2])
    own_v = pltpu.make_async_copy(v.at[:, :, columns(g)], kv.at[c, spot, 1], load_sem.at[3])
    own_k.start()
    own_v.start()
    pltpu.make_async_copy(q.at[:, columns(me)], qb.at[me], q_sem.at[z]).start()

    def near_out(chip):
        group = lax.div(chip, 2)
        place = lax.rem(z - 2 * group - 1 + 2 * CHIPS, CHIPS)
        for part, source in enumerate((k, v)):
            remote(
                source.at[:, :, columns(group)],
                kv.at[c, place, part],
                near_send_sem.at[0],
                near_sem.at[0],
                2 * chip + c,
            ).start()

    def picked(head):
        block = jnp.int32(0)
        count = vc[head]
        for t in range(DEV):
            entry = vb[head, t]
            mine = (lax.shift_right_logical(entry, 3) == me) & (t < count)
            block = block + jnp.where(mine, entry - OWN * me, 0)
        return block

    def pick(head, buffer, slot):
        block = picked(head)
        cols = columns(lax.div(head, H // KVH))
        buffer[slot, 0] = pkb[block, :, cols]
        buffer[slot, 1] = pvb[block, :, cols]

    def far_out(head):
        pick(head, far_send, head)
        remote(far_send.at[head], far.at[me], far_send_sem, far_sem, head).start()

    pl.semaphore_wait(barrier, 4 * RADIUS + 1)

    def serve(distance, carry):
        ahead = lax.rem(z + distance, CHIPS)
        behind = lax.rem(z + CHIPS - distance, CHIPS)

        @pl.when(lax.rem(ahead, 2) == 0)
        def _():
            near_out(ahead)

        @pl.when(lax.rem(behind, 2) == 1)
        def _():
            near_out(behind)

        return carry

    done, reach, rounds = 0, RADIUS, 0
    while reach < CHIPS // 2:
        for chip in (lax.rem(z + reach, CHIPS), lax.rem(z + CHIPS - reach, CHIPS)):
            signal(known_sem.at[rounds], 2 * chip + c)
        lax.fori_loop(done + 1, reach + 1, serve, 0)
        pl.semaphore_wait(known_sem.at[rounds], 2)
        done, reach, rounds = reach, 2 * reach, rounds + 1
    for distance in range(CHIPS // 2 - 1, done, -1):
        serve(distance, 0)
    for copy in metas:
        copy.wait()
    load_k.wait()
    load_v.wait()

    def far_step(t, carry):
        chip = lax.rem(z + mixed(t) + CHIPS, CHIPS)
        for core in range(2):

            @pl.when(2 * chip + core != me)
            def _():
                far_out(2 * chip + core)

        return carry

    lax.fori_loop(0, CHIPS, far_step, 0)
    pick(me, far, me)

    own_k.wait()
    own_v.wait()
    first = OWN * (1 - odd)
    other = OWN * odd
    mine = kv.at[c, pl.ds(first, OWN)]
    wait_bytes(kv.at[c, pl.ds(first, OWN - 1)], near_sem.at[0])
    remote(mine, mine, near_send_sem.at[2], near_sem.at[2], across).start()
    remote(mine, mine, near_send_sem.at[1], near_sem.at[1], sibling).start()

    def q_out(t, carry):
        chip = lax.rem(z - mixed(t) + CHIPS, CHIPS)
        for core in range(2):
            device = 2 * chip + core

            @pl.when(device != me)
            def _():
                remote(
                    q.at[:, columns(device)], qb.at[me], q_send_sem, q_sem.at[z], device
                ).start()

        return carry

    lax.fori_loop(0, 16, q_out, 0)

    count = vc[me]
    lane = lax.broadcasted_iota(jnp.int32, (1, FAR), 1)
    slot = lax.shift_right_logical(lane, 6)
    live = jnp.zeros((1, FAR), jnp.int32)
    for t in range(DEV):
        owner = jnp.where(t < count, lax.shift_right_logical(vb[me, t], 3), -1)
        live = jnp.where(slot == owner, 1, live)
    far_bias[...] = jnp.where(live > 0, 0.0, NEG)
    key = lax.broadcasted_iota(jnp.int32, (BLK, NEAR), 1)
    row = lax.broadcasted_iota(jnp.int32, (BLK, NEAR), 0)
    tri[...] = jnp.where((key < BLK) & (key > row), NEG, 0.0)

    theirs = kv.at[c, pl.ds(other, OWN)]
    wait_bytes(theirs, near_sem.at[2])
    remote(theirs, theirs, near_send_sem.at[3], near_sem.at[3], sibling).start()

    wait_bytes(far_send.at[pl.ds(0, DEV - 1)], far_sem)
    wait_bytes(mine, near_sem.at[1])
    wait_bytes(theirs, near_sem.at[3])

    near_slot = lax.shift_right_logical(lax.broadcasted_iota(jnp.int32, (1, NEAR), 1), 6)
    nt = (((1,), (1,)), ((), ()))
    nn = (((1,), (0,)), ((), ()))

    def step(t, carry):
        chip = lax.rem(z + turn(t) + CHIPS, CHIPS)
        wait_bytes(qb.at[pl.ds(2 * chip, 2)], q_sem.at[chip])
        rows = qb[pl.ds(2 * chip, 2)].reshape(2 * TOK, HD)
        far_keys = far[:, 0].reshape(FAR, HD)
        far_values = far[:, 1].reshape(FAR, HD)
        far_scores = lax.dot_general(rows, far_keys, nt, preferred_element_type=jnp.float32)
        far_scores = far_scores + far_bias[...]
        far_top = jnp.max(far_scores, 1, keepdims=True)
        tops, near_scores, near_values = [], [], []
        for b in range(4):
            block = 4 * chip + b
            keys, values = [], []
            bias = jnp.zeros((1, NEAR), jnp.float32)
            for s in range(SMAX):
                offset = so[s, me]
                target = jnp.maximum(block - offset, 0)
                their_chip = lax.shift_right_logical(target, 2)
                core = lax.shift_right_logical(target, 1) & 1
                place = (their_chip - 2 * g - 1) & (CHIPS - 1)
                half = target & 1
                keys.append(kv[core, place, 0, half])
                values.append(kv[core, place, 1, half])
                seen = (block >= offset) & (s < sc[me])
                bias = jnp.where(near_slot == s, jnp.where(seen, 0.0, NEG), bias)
            scores = lax.dot_general(
                rows[b * BLK : (b + 1) * BLK],
                jnp.concatenate(keys, 0),
                nt,
                preferred_element_type=jnp.float32,
            )
            scores = scores + (tri[...] + bias)
            near_scores.append(scores)
            near_values.append(jnp.concatenate(values, 0))
            tops.append(jnp.max(scores, 1, keepdims=True))
        top = jnp.maximum(far_top, jnp.concatenate(tops, 0)) * SCALE
        far_weights = jnp.exp2(far_scores * SCALE - top)
        total = jnp.sum(far_weights, 1, keepdims=True)
        mixed = lax.dot_general(
            far_weights.astype(jnp.bfloat16), far_values, nn, preferred_element_type=jnp.float32
        )
        for b in range(4):
            own = slice(b * BLK, (b + 1) * BLK)
            weights = jnp.exp2(near_scores[b] * SCALE - top[own])
            sums = total[own] + jnp.sum(weights, 1, keepdims=True)
            near_mixed = lax.dot_general(
                weights.astype(jnp.bfloat16),
                near_values[b],
                nn,
                preferred_element_type=jnp.float32,
            )
            done = (mixed[own] + near_mixed) / sums
            ob[2 * chip + b // 2, pl.ds((b % 2) * BLK, BLK), :] = done.astype(jnp.bfloat16)
        for core in range(2):
            device = 2 * chip + core

            @pl.when(device == me)
            def _():
                pltpu.make_async_copy(ob.at[device], out.at[:, columns(me)], out_sem).start()

            @pl.when(device != me)
            def _():
                remote(
                    ob.at[device], out.at[:, columns(me)], out_send_sem, out_sem, device
                ).start()

        return carry

    lax.fori_loop(0, CHIPS, step, 0)

    wait_bytes(ob, out_sem)
    most = ob.at[pl.ds(0, DEV - 1)]
    wait_bytes(most, out_send_sem)
    wait_bytes(most, q_send_sem)
    wait_bytes(far_send.at[pl.ds(0, DEV - 1)], far_send_sem)
    wait_bytes(kv.at[0, pl.ds(0, KVH - 1)], near_send_sem.at[0])
    wait_bytes(mine, near_send_sem.at[1])
    wait_bytes(mine, near_send_sem.at[2])
    wait_bytes(theirs, near_send_sem.at[3])


def shards(q, k, v, pk, pv, vb, vc, so, sc):
    hbm = pl.BlockSpec(memory_space=pl.ANY)
    dma = pltpu.SemaphoreType.DMA
    bf16 = jnp.bfloat16
    return pl.pallas_call(
        kernel,
        out_shape=pltpu.VMEM((TOK, H * HD), bf16),
        in_specs=[hbm] * 9,
        out_specs=pl.BlockSpec(memory_space=pltpu.VMEM),
        scratch_shapes=[
            pltpu.VMEM((2, CHIPS, 2, 2, BLK, HD), bf16),
            pltpu.VMEM((DEV, 2, BLK, HD), bf16),
            pltpu.VMEM((DEV, 2, BLK, HD), bf16),
            pltpu.VMEM((OWN, BLK, KVH * HD), bf16),
            pltpu.VMEM((OWN, BLK, KVH * HD), bf16),
            pltpu.VMEM((DEV, TOK, HD), bf16),
            pltpu.VMEM((DEV, TOK, HD), bf16),
            pltpu.VMEM((1, FAR), jnp.float32),
            pltpu.VMEM((BLK, NEAR), jnp.float32),
            pltpu.SMEM((DEV, DEV), jnp.int32),
            pltpu.SMEM((DEV,), jnp.int32),
            pltpu.SMEM((SMAX, DEV), jnp.int32),
            pltpu.SMEM((DEV,), jnp.int32),
            dma((8,)),
            dma((4,)),
            dma((4,)),
            dma,
            dma,
            dma((CHIPS,)),
            dma,
            dma,
            dma,
            pltpu.SemaphoreType.REGULAR((4,)),
        ],
        compiler_params=pltpu.CompilerParams(
            collective_id=0, has_side_effects=True, vmem_limit_bytes=60 << 20
        ),
    )(
        q,
        k.reshape(2, BLK, KVH * HD),
        v.reshape(2, BLK, KVH * HD),
        pk.reshape(OWN, BLK, KVH * HD),
        pv.reshape(OWN, BLK, KVH * HD),
        vb,
        vc,
        so.T,
        sc,
    )


def solution(mesh):
    tokens = P(("req", "head"), None)
    return jax.shard_map(
        shards,
        mesh=mesh,
        in_specs=(tokens,) * 5 + (P("req", None), P("req"), P("req", None), P("req")),
        out_specs=tokens,
        check_vma=False,
    )
```
